768 devices in a mesh: wide: 64 (over x, y, core), narrow: 12 (over z).
Axes of the slice: x: 4, y: 8, z: 12, core: 2. Of those that a mesh axis runs over, the one named last changes fastest.
Arguments:
- integrals: bfloat16 [6144, 64, 4096], P(('wide', 'narrow')), may hold values from -0.09375 to 0.09375
- task_shape: int32 [6144], P(('wide', 'narrow')), may hold values from 16 to 64
- task_rows: int32 [6144], P(('wide', 'narrow')), may hold values from 0 to 11
- task_cols: int32 [6144], P(('wide', 'narrow')), may hold values from 0 to 63
- tile_owner: int32 [64], replicated, may hold values from 0 to 63, each once
- amplitudes: bfloat16 [64, 16, 4096], P('wide'), may hold values from -6 to 6
Outputs:
- ladder: float32 [16, 49152], P(None, ('wide', 'narrow'))
The draws below stay inside these ranges and needn't reach their ends.
Inputs may be any that keep to these rules, and one draw needn't show every extreme that they name: `tile_owner`: each slot once.
All inputs are finite; a program needn't handle non-finite values.
Results may differ from the reference program's by a relative error of at most 0.0003.
Values may be sent and summed in bfloat16 or wider, within the bound.
No kernel may reach another device: no remote copies, remote signals or barrier semaphores. Data moves between devices by JAX's collectives and lax.ppermute only.
A program may use at most 32 MiB of HBM per device.

```python
import jax
import jax.numpy as jnp
from jax import lax

TW = 64
PAIRS = 16
TASK_DEV = 8
NTASK = 6144
NT2 = 64
GROUP_ROWS = 12
NROWT = 768
N_NARROW = 12


def plant(values, key, low, high):
    extent = values.shape
    spot = [jax.random.randint(jax.random.fold_in(key, axis), (), 0, extent[axis]) for axis in range(len(extent))]
    values = values.at[tuple(spot)].set(low)
    longest = extent.index(max(extent))
    spot[longest] = (spot[longest] + 1) % extent[longest]
    return values.at[tuple(spot)].set(high)


def steps_of(stream_key, extent, pieces, low, largest):
    factor_of, own = 1.0, jax.random.fold_in(stream_key, 6)
    for dim, blocks in pieces:
        draws = jnp.exp(jax.random.uniform(jax.random.fold_in(own, dim), (blocks,), jnp.float32, low / len(pieces), largest / len(pieces)))
        factor_of = factor_of * jnp.repeat(draws, extent[dim] // blocks).reshape([-1 if axis == dim else 1 for axis in range(len(extent))])
    return factor_of


def bell_draw(own_key, shape, width, reach, split=(), kind=jnp.bfloat16):
    array = width * jax.random.normal(own_key, shape, jnp.float32)
    if split:
        array = array * steps_of(own_key, shape, split, -0.22, 0.18)
    return jnp.clip(array, -reach, reach).astype(kind)


def setup_inputs(seed: int = 0) -> dict:
    splits = jax.random.split(jax.random.key(seed), 7)
    return {
        "integrals": bell_draw(splits[0], (NTASK, TW, TW * TW), (TW * TW) ** -0.5, 0.09375, ((0, 768),)),
        "task_shape": plant(jax.random.randint(splits[1], (NTASK,), TW // 4, TW + 1), jax.random.fold_in(splits[1], 1), TW // 4, TW).astype(jnp.int32),
        "task_rows": plant(jax.random.randint(splits[2], (NTASK,), 0, GROUP_ROWS), jax.random.fold_in(splits[2], 1), 0, GROUP_ROWS - 1).astype(jnp.int32),
        "task_cols": plant(jax.random.randint(splits[3], (NTASK,), 0, NT2), jax.random.fold_in(splits[3], 1), 0, NT2 - 1).astype(jnp.int32),
        "tile_owner": jax.random.permutation(splits[4], NT2).astype(jnp.int32),
        "amplitudes": bell_draw(splits[5], (NT2, PAIRS, TW * TW), 1.0, 6.0, ((0, 64),)),
    }


def reference(integrals, task_shape, task_rows, task_cols, tile_owner, amplitudes):
    slot_ids = jnp.take(tile_owner, task_cols, axis=0).astype(jnp.int32)
    group_ids = ((jnp.arange(NTASK, dtype=jnp.int32) // TASK_DEV) // N_NARROW).astype(jnp.int32)
    block_ids = (group_ids * GROUP_ROWS + task_rows).astype(jnp.int32)

    def per_block(first_task):
        tiles = lax.dynamic_slice_in_dim(integrals, first_task, TASK_DEV, 0).astype(jnp.float32)
        wanted = lax.dynamic_slice_in_dim(slot_ids, first_task, TASK_DEV, 0)
        chosen = jnp.take(amplitudes, wanted, axis=0).astype(jnp.float32)
        partial_value = jnp.einsum("tbx,tpx->tpb", tiles, chosen, precision=lax.Precision.HIGHEST)
        shapes = lax.dynamic_slice_in_dim(task_shape, first_task, TASK_DEV, 0)
        live_rows = jnp.arange(TW, dtype=jnp.int32)[None, :] < shapes[:, None]
        return jnp.where(live_rows[:, None, :], partial_value, jnp.zeros_like(partial_value))

    starts = jnp.arange(NTASK // TASK_DEV, dtype=jnp.int32) * TASK_DEV
    partials = lax.map(per_block, starts).reshape(NTASK, PAIRS, TW)
    result = jnp.zeros((NROWT, PAIRS, TW), jnp.float32).at[block_ids].add(partials)
    return jnp.transpose(result, (1, 0, 2)).reshape(PAIRS, NROWT * TW)
```

```python
import jax
import jax.numpy as jnp
from jax import lax
from jax.sharding import PartitionSpec as P

XS, YH, YL, CORES = 4, 4, 2, 2
GROUP = XS * YL * CORES
LANES = 128


def local(integrals, task_shape, task_rows, task_cols, tile_owner, amplitudes):
    tasks, tile_width, depth = integrals.shape
    pairs = amplitudes.shape[1]
    narrow = lax.axis_size("narrow")
    wide = lax.axis_size("wide")
    part = depth // GROUP
    halves = part // LANES
    payload = halves * pairs
    groups = [
        [((x * YH + yh) * YL + yl) * CORES + c for x in range(XS) for yl in range(YL) for c in range(CORES)]
        for yh in range(YH)
    ]

    slots = jnp.take(tile_owner, task_cols, axis=0)
    slices = amplitudes.reshape(pairs, GROUP, halves, LANES).transpose(1, 2, 0, 3)
    slices = slices.reshape(GROUP, payload, LANES)
    wanted = jnp.broadcast_to(slots.astype(amplitudes.dtype)[None, :, None], (GROUP, tasks, LANES))
    blocks = jnp.concatenate([slices, wanted], axis=1)
    blocks = blocks.reshape(XS, 1, YL, CORES, payload + tasks, LANES)
    blocks = jnp.broadcast_to(blocks, (XS, YH, YL, CORES, payload + tasks, LANES))
    blocks = blocks.reshape(wide, payload + tasks, LANES)
    have = lax.all_to_all(blocks, "wide", 0, 0, tiled=True)

    yh = (lax.axis_index("wide") // (YL * CORES)) % YH
    asked = have[:, payload:, 0].reshape(XS, YH, YL * CORES, tasks)
    asked = lax.dynamic_index_in_dim(asked, yh, 1, keepdims=False).reshape(GROUP * tasks)
    chosen = jnp.take(have[:, :payload], asked.astype(jnp.int32), axis=0)
    chosen = chosen.reshape(GROUP, tasks * payload, LANES)
    needed = lax.all_to_all(chosen, "wide", 0, 0, axis_index_groups=groups, tiled=True)
    needed = needed.reshape(GROUP, tasks, halves, pairs, LANES).transpose(1, 3, 0, 2, 4)
    needed = needed.reshape(tasks, pairs, depth)

    partial = jnp.einsum("tbx,tpx->tpb", integrals, needed, preferred_element_type=jnp.float32)
    live = lax.broadcasted_iota(jnp.int32, (tasks, tile_width), 1) < task_shape[:, None]
    partial = jnp.where(live[:, None, :], partial, 0.0)
    one_hot = (task_rows[:, None] == lax.broadcasted_iota(jnp.int32, (tasks, narrow), 1)).astype(jnp.float32)
    rows = jnp.einsum("tr,tpb->rpb", one_hot, partial, precision=lax.Precision.HIGHEST)
    rows = lax.all_to_all(rows, "narrow", 0, 0, tiled=True)
    return jnp.sum(rows, axis=0)


def solution(mesh):
    placed = (
        P(("wide", "narrow"), None, None),
        P(("wide", "narrow")),
        P(("wide", "narrow")),
        P(("wide", "narrow")),
        P(),
        P("wide", None, None),
    )
    return jax.shard_map(
        local, mesh=mesh, in_specs=placed, out_specs=P(None, ("wide", "narrow")), check_vma=False
    )
```

```python
import jax
import jax.numpy as jnp
from jax import lax
from jax.experimental import pallas as pl
from jax.experimental.pallas import tpu as pltpu
from jax.sharding import PartitionSpec as P

XS, YH, YL, CORES = 4, 4, 2, 2
NEAR = YL * CORES
GROUP = XS * NEAR
LANES = 128
VMEM = pl.BlockSpec(memory_space=pltpu.VMEM)
SMEM = pl.BlockSpec(memory_space=pltpu.SMEM)


def spread_kernel(cols_ref, owner_ref, amp_ref, out_ref):
    tasks = cols_ref.shape[0]
    _, pairs, depth = amp_ref.shape
    part = depth // GROUP
    payload = part // LANES * pairs
    rows = out_ref.shape[1] - payload
    lane = lax.broadcasted_iota(jnp.int32, (rows, LANES), 1)
    wanted = jnp.zeros((rows, LANES), jnp.float32)
    for s in range(tasks):
        wanted = jnp.where(lane == s, owner_ref[cols_ref[s]].astype(jnp.float32), wanted)
    wanted = wanted.astype(out_ref.dtype)
    for j in range(GROUP):
        x, near = divmod(j, NEAR)
        for yh in range(YH):
            w = (x * YH + yh) * NEAR + near
            for h in range(part // LANES):
                at = j * part + h * LANES
                out_ref[w, h * pairs : (h + 1) * pairs, :] = amp_ref[0, :, at : at + LANES]
            out_ref[w, payload:, :] = wanted


def select_kernel(asked_ref, have_ref, out_ref):
    payload = out_ref.shape[1]

    def copy(i, carry):
        out_ref[i] = have_ref[asked_ref[i], :payload, :]
        return carry

    lax.fori_loop(0, out_ref.shape[0], copy, 0, unroll=8)


def ladder_kernel(shape_ref, rows_ref, integrals_ref, needed_ref, out_ref, weight_ref):
    step, steps = pl.program_id(0), pl.num_programs(0)
    some, width, depth = integrals_ref.shape
    tasks = shape_ref.shape[0]
    members, per, _ = needed_ref.shape
    halves = depth // members // LANES
    pairs = per // tasks // halves

    @pl.when(step == 0)
    def _():
        out_ref[...] = jnp.zeros_like(out_ref)
        for s in range(tasks):
            for j in range(members):
                for h in range(halves):
                    at = (j * halves + h) * LANES
                    row = (s * halves + h) * pairs
                    weight_ref[s, :, at : at + LANES] = needed_ref[j, row : row + pairs, :]

    for i in range(some):
        t = step * some + i
        product = lax.dot_general(
            weight_ref[t], integrals_ref[i], (((1,), (1,)), ((), ())), preferred_element_type=jnp.float32
        )
        live = lax.broadcasted_iota(jnp.int32, product.shape, 1) < shape_ref[t]
        product = jnp.where(live, product, 0.0)
        packed = jnp.concatenate([product[: pairs // 2], product[pairs // 2 :]], axis=1)
        out_ref[rows_ref[t]] += packed


def local(integrals, task_shape, task_rows, task_cols, tile_owner, amplitudes):
    tasks, width, depth = integrals.shape
    pairs = amplitudes.shape[1]
    narrow = lax.axis_size("narrow")
    wide = lax.axis_size("wide")
    payload = depth // GROUP // LANES * pairs
    kind = amplitudes.dtype
    groups = [[(x * YH + yh) * NEAR + near for x in range(XS) for near in range(NEAR)] for yh in range(YH)]

    blocks = pl.pallas_call(
        spread_kernel,
        out_shape=jax.ShapeDtypeStruct((wide, payload + 8, LANES), kind),
        in_specs=[SMEM, SMEM, VMEM],
        out_specs=VMEM,
    )(task_cols, tile_owner, amplitudes)
    have = lax.all_to_all(blocks, "wide", 0, 0, tiled=True)

    yh = lax.div(lax.axis_index("wide"), NEAR) % YH
    asked = have[:, payload, :tasks].reshape(XS, YH, NEAR, tasks)
    asked = lax.dynamic_index_in_dim(asked, yh, 1, keepdims=False).reshape(GROUP * tasks)
    chosen = pl.pallas_call(
        select_kernel,
        out_shape=jax.ShapeDtypeStruct((GROUP * tasks, payload, LANES), kind),
        in_specs=[SMEM, VMEM],
        out_specs=VMEM,
    )(asked.astype(jnp.int32), have)
    chosen = chosen.reshape(GROUP, tasks * payload, LANES)
    needed = lax.all_to_all(chosen, "wide", 0, 0, axis_index_groups=groups, tiled=True)

    some = 2
    rows = pl.pallas_call(
        ladder_kernel,
        out_shape=jax.ShapeDtypeStruct((narrow, pairs // 2, 2 * width), jnp.float32),
        grid_spec=pltpu.PrefetchScalarGridSpec(
            num_scalar_prefetch=2,
            grid=(tasks // some,),
            in_specs=[
                pl.BlockSpec((some, width, depth), lambda i, *_: (i, 0, 0)),
                pl.BlockSpec(needed.shape, lambda i, *_: (0, 0, 0)),
            ],
            out_specs=pl.BlockSpec((narrow, pairs // 2, 2 * width), lambda i, *_: (0, 0, 0)),
            scratch_shapes=[pltpu.VMEM((tasks, pairs, depth), kind)],
        ),
        compiler_params=pltpu.CompilerParams(vmem_limit_bytes=32 * 1024 * 1024),
    )(task_shape, task_rows, integrals, needed)
    rows = lax.all_to_all(rows, "narrow", 0, 0, tiled=True)
    total = jnp.sum(rows, axis=0)
    return jnp.concatenate([total[:, :width], total[:, width:]], axis=0)


def solution(mesh):
    placed = (
        P(("wide", "narrow"), None, None),
        P(("wide", "narrow")),
        P(("wide", "narrow")),
        P(("wide", "narrow")),
        P(),
        P("wide", None, None),
    )
    return jax.shard_map(
        local, mesh=mesh, in_specs=placed, out_specs=P(None, ("wide", "narrow")), check_vma=False
    )
```

```python
import jax
import jax.numpy as jnp
from jax import lax
from jax.experimental import pallas as pl
from jax.experimental.pallas import tpu as pltpu
from jax.sharding import PartitionSpec as P

XS, YH, YL, CORES = 4, 4, 2, 2
NEAR = YL * CORES
GROUP = XS * NEAR
LANES = 128
VMEM = pl.BlockSpec(memory_space=pltpu.VMEM)
SMEM = pl.BlockSpec(memory_space=pltpu.SMEM)


def room(mib):
    return pltpu.CompilerParams(vmem_limit_bytes=mib * 1024 * 1024)


def spread_kernel(cols_ref, owner_ref, amp_ref, out_ref):
    tasks = cols_ref.shape[0]
    _, pairs, depth = amp_ref.shape
    part = depth // GROUP
    payload = part // LANES * pairs
    rows = out_ref.shape[1] - payload
    lane = lax.broadcasted_iota(jnp.int32, (rows, LANES), 1)
    wanted = jnp.zeros((rows, LANES), jnp.float32)
    for s in range(tasks):
        wanted = jnp.where(lane == s, owner_ref[cols_ref[s]].astype(jnp.float32), wanted)
    wanted = wanted.astype(out_ref.dtype)
    for j in range(GROUP):
        x, near = divmod(j, NEAR)
        for yh in range(YH):
            w = (x * YH + yh) * NEAR + near
            for h in range(part // LANES):
                at = j * part + h * LANES
                out_ref[w, h * pairs : (h + 1) * pairs, :] = amp_ref[0, :, at : at + LANES]
            out_ref[w, payload:, :] = wanted


def select_kernel(asked_ref, have_ref, out_ref):
    payload = out_ref.shape[1]

    def copy(i, carry):
        out_ref[i] = have_ref[asked_ref[i], :payload, :]
        return carry

    lax.fori_loop(0, out_ref.shape[0], copy, 0, unroll=8)


def ladder_kernel(shape_ref, rows_ref, integrals_ref, needed_ref, out_ref):
    tasks, width, depth = integrals_ref.shape
    members, per, _ = needed_ref.shape
    halves = depth // members // LANES
    pairs = per // tasks // halves
    out_ref[...] = jnp.zeros_like(out_ref)
    for t in range(tasks):
        chosen = [
            needed_ref[j, (t * halves + h) * pairs : (t * halves + h + 1) * pairs, :]
            for j in range(members)
            for h in range(halves)
        ]
        product = lax.dot_general(
            jnp.concatenate(chosen, axis=1),
            integrals_ref[t],
            (((1,), (1,)), ((), ())),
            preferred_element_type=jnp.float32,
        )
        live = lax.broadcasted_iota(jnp.int32, product.shape, 1) < shape_ref[t]
        product = jnp.where(live, product, 0.0)
        out_ref[rows_ref[t]] += jnp.concatenate([product[: pairs // 2], product[pairs // 2 :]], axis=1)


def local(integrals, task_shape, task_rows, task_cols, tile_owner, amplitudes):
    tasks, width, depth = integrals.shape
    pairs = amplitudes.shape[1]
    narrow = lax.axis_size("narrow")
    wide = lax.axis_size("wide")
    payload = depth // GROUP // LANES * pairs
    kind = amplitudes.dtype
    groups = [[(x * YH + yh) * NEAR + near for x in range(XS) for near in range(NEAR)] for yh in range(YH)]

    blocks = pl.pallas_call(
        spread_kernel,
        out_shape=jax.ShapeDtypeStruct((wide, payload + 8, LANES), kind),
        in_specs=[SMEM, SMEM, VMEM],
        out_specs=VMEM,
        compiler_params=room(2),
    )(task_cols, tile_owner, amplitudes)
    have = lax.all_to_all(blocks, "wide", 0, 0, tiled=True)

    yh = lax.div(lax.axis_index("wide"), NEAR) % YH
    asked = have[:, payload, :tasks].reshape(XS, YH, NEAR, tasks)
    asked = lax.dynamic_index_in_dim(asked, yh, 1, keepdims=False).reshape(GROUP * tasks)
    chosen = pl.pallas_call(
        select_kernel,
        out_shape=jax.ShapeDtypeStruct((GROUP * tasks, payload, LANES), kind),
        in_specs=[SMEM, VMEM],
        out_specs=VMEM,
        compiler_params=room(3),
    )(asked.astype(jnp.int32), have)
    chosen = chosen.reshape(GROUP, tasks * payload, LANES)
    needed = lax.all_to_all(chosen, "wide", 0, 0, axis_index_groups=groups, tiled=True)

    rows = pl.pallas_call(
        ladder_kernel,
        out_shape=jax.ShapeDtypeStruct((narrow, pairs // 2, 2 * width), jnp.float32),
        in_specs=[SMEM, SMEM, VMEM, VMEM],
        out_specs=VMEM,
        compiler_params=room(6),
    )(task_shape, task_rows, integrals, needed)
    rows = lax.all_to_all(rows, "narrow", 0, 0, tiled=True)
    total = jnp.sum(rows, axis=0)
    return jnp.concatenate([total[:, :width], total[:, width:]], axis=0)


def solution(mesh):
    placed = (
        P(("wide", "narrow"), None, None),
        P(("wide", "narrow")),
        P(("wide", "narrow")),
        P(("wide", "narrow")),
        P(),
        P("wide", None, None),
    )
    return jax.shard_map(
        local, mesh=mesh, in_specs=placed, out_specs=P(None, ("wide", "narrow")), check_vma=False
    )
```

```python
import jax
import jax.numpy as jnp
from jax import lax
from jax.experimental import pallas as pl
from jax.experimental.pallas import tpu as pltpu
from jax.sharding import PartitionSpec as P

XS, YH, YL, CORES = 4, 4, 2, 2
NEAR = YL * CORES
GROUP = XS * NEAR
LANES = 128
ANY = pl.BlockSpec(memory_space=pl.ANY)
VMEM = pl.BlockSpec(memory_space=pltpu.VMEM)
SMEM = pl.BlockSpec(memory_space=pltpu.SMEM)


def room(mib):
    return pltpu.CompilerParams(vmem_limit_bytes=mib * 1024 * 1024)


def stay(x):
    return pltpu.with_memory_space_constraint(x, pltpu.HBM)


def keep(x):
    return pltpu.with_memory_space_constraint(x, pltpu.VMEM)


def spread_kernel(cols_hbm, owner_hbm, amp_hbm, out_ref, cols_ref, owner_ref, amp_ref, sems):
    pairs_of = ((cols_hbm, cols_ref), (owner_hbm, owner_ref), (amp_hbm, amp_ref))
    copies = [pltpu.make_async_copy(src, dst, sems.at[i]) for i, (src, dst) in enumerate(pairs_of)]
    for copy in copies:
        copy.start()
    tasks = cols_ref.shape[0]
    _, pairs, depth = amp_ref.shape
    part = depth // GROUP
    payload = part // LANES * pairs
    rows = out_ref.shape[1] - payload
    copies[0].wait()
    copies[1].wait()
    lane = lax.broadcasted_iota(jnp.int32, (rows, LANES), 1)
    wanted = jnp.zeros((rows, LANES), jnp.float32)
    for s in range(tasks):
        wanted = jnp.where(lane == s, owner_ref[cols_ref[s]].astype(jnp.float32), wanted)
    wanted = wanted.astype(out_ref.dtype)
    copies[2].wait()
    for j in range(GROUP):
        x, near = divmod(j, NEAR)
        for yh in range(YH):
            w = (x * YH + yh) * NEAR + near
            for h in range(part // LANES):
                at = j * part + h * LANES
                out_ref[w, h * pairs : (h + 1) * pairs, :] = amp_ref[0, :, at : at + LANES]
            out_ref[w, payload:, :] = wanted


def select_kernel(asked_ref, have_ref, out_ref):
    payload = out_ref.shape[1]
    tasks = out_ref.shape[0] // GROUP
    yh = lax.rem(lax.div(lax.axis_index("wide"), NEAR), YH)
    for j in range(GROUP):
        x, near = divmod(j, NEAR)
        w = (x * YH + yh) * NEAR + near
        for s in range(tasks):
            out_ref[j * tasks + s] = have_ref[asked_ref[w * tasks + s], :payload, :]


def ladder_kernel(shape_ref, rows_ref, integrals_ref, needed_ref, out_ref):
    tasks, width, depth = integrals_ref.shape
    members, per, _ = needed_ref.shape
    halves = depth // members // LANES
    pairs = per // tasks // halves
    out_ref[...] = jnp.zeros_like(out_ref)
    for t in range(tasks):
        chosen = [
            needed_ref[j, (t * halves + h) * pairs : (t * halves + h + 1) * pairs, :]
            for j in range(members)
            for h in range(halves)
        ]
        product = lax.dot_general(
            jnp.concatenate(chosen, axis=1),
            integrals_ref[t],
            (((1,), (1,)), ((), ())),
            preferred_element_type=jnp.float32,
        )
        live = lax.broadcasted_iota(jnp.int32, product.shape, 1) < shape_ref[t]
        product = jnp.where(live, product, 0.0)
        out_ref[rows_ref[t]] += jnp.concatenate([product[: pairs // 2], product[pairs // 2 :]], axis=1)


def local(integrals, task_shape, task_rows, task_cols, tile_owner, amplitudes):
    tasks, width, depth = integrals.shape
    pairs = amplitudes.shape[1]
    narrow = lax.axis_size("narrow")
    wide = lax.axis_size("wide")
    payload = depth // GROUP // LANES * pairs
    kind = amplitudes.dtype
    groups = [[(x * YH + yh) * NEAR + near for x in range(XS) for near in range(NEAR)] for yh in range(YH)]

    blocks = pl.pallas_call(
        spread_kernel,
        out_shape=jax.ShapeDtypeStruct((wide, payload + 8, LANES), kind),
        in_specs=[ANY, ANY, ANY],
        out_specs=VMEM,
        scratch_shapes=[
            pltpu.SMEM(task_cols.shape, jnp.int32),
            pltpu.SMEM(tile_owner.shape, jnp.int32),
            pltpu.VMEM(amplitudes.shape, kind),
            pltpu.SemaphoreType.DMA((3,)),
        ],
        compiler_params=room(1),
    )(stay(task_cols), stay(tile_owner), stay(amplitudes))
    have = lax.all_to_all(blocks, "wide", 0, 0, tiled=True)

    asked = have[:, payload, :tasks].astype(jnp.int32).reshape(wide * tasks)
    chosen = pl.pallas_call(
        select_kernel,
        out_shape=jax.ShapeDtypeStruct((GROUP * tasks, payload, LANES), kind),
        in_specs=[SMEM, VMEM],
        out_specs=VMEM,
        compiler_params=room(3),
    )(asked, have)
    chosen = chosen.reshape(GROUP, tasks * payload, LANES)
    needed = lax.all_to_all(chosen, "wide", 0, 0, axis_index_groups=groups, tiled=True)

    rows = pl.pallas_call(
        ladder_kernel,
        out_shape=jax.ShapeDtypeStruct((narrow, pairs // 2, 2 * width), jnp.float32),
        in_specs=[SMEM, SMEM, VMEM, VMEM],
        out_specs=VMEM,
        compiler_params=room(1),
    )(task_shape, task_rows, integrals, needed)
    rows = lax.all_to_all(rows, "narrow", 0, 0, tiled=True)
    total = jnp.sum(rows, axis=0)
    return jnp.concatenate([total[:, :width], total[:, width:]], axis=0)


def solution(mesh):
    placed = (
        P(("wide", "narrow"), None, None),
        P(("wide", "narrow")),
        P(("wide", "narrow")),
        P(("wide", "narrow")),
        P(),
        P("wide", None, None),
    )
    return jax.shard_map(
        local, mesh=mesh, in_specs=placed, out_specs=P(None, ("wide", "narrow")), check_vma=False
    )
```

```python
import jax
import jax.numpy as jnp
from jax import lax
from jax.experimental import pallas as pl
from jax.experimental.pallas import tpu as pltpu
from jax.sharding import PartitionSpec as P

XS, YH, YL, CORES = 4, 4, 2, 2
NEAR = YL * CORES
GROUP = XS * NEAR
LANES = 128
ANY = pl.BlockSpec(memory_space=pl.ANY)
VMEM = pl.BlockSpec(memory_space=pltpu.VMEM)
SMEM = pl.BlockSpec(memory_space=pltpu.SMEM)


def room(mib):
    return pltpu.CompilerParams(vmem_limit_bytes=mib * 1024 * 1024)


def stay(x):
    return pltpu.with_memory_space_constraint(x, pltpu.HBM)


def keep(x):
    return pltpu.with_memory_space_constraint(x, pltpu.VMEM)


def spread_kernel(cols_hbm, owner_hbm, amp_hbm, out_ref, cols_ref, owner_ref, amp_ref, sems):
    pairs_of = ((cols_hbm, cols_ref), (owner_hbm, owner_ref), (amp_hbm, amp_ref))
    copies = [pltpu.make_async_copy(src, dst, sems.at[i]) for i, (src, dst) in enumerate(pairs_of)]
    for copy in copies:
        copy.start()
    tasks = cols_ref.shape[0]
    _, pairs, depth = amp_ref.shape
    part = depth // GROUP
    payload = out_ref.shape[1] - 1
    copies[0].wait()
    copies[1].wait()
    lane = lax.broadcasted_iota(jnp.int32, (2, LANES), 1)
    wanted = jnp.zeros((2, LANES), jnp.float32)
    for s in range(tasks):
        wanted = jnp.where(lane == s, owner_ref[cols_ref[s]].astype(jnp.float32), wanted)
    wanted = wanted.astype(out_ref.dtype)
    copies[2].wait()
    for j in range(GROUP):
        x, near = divmod(j, NEAR)
        for h in range(part // LANES):
            at = j * part + h * LANES
            tile = amp_ref[0, :, at : at + LANES].reshape(pairs // 2, 2, LANES)
            for yh in range(YH):
                out_ref[(x * YH + yh) * NEAR + near, h * (pairs // 2) : (h + 1) * (pairs // 2)] = tile
        for yh in range(YH):
            out_ref[(x * YH + yh) * NEAR + near, payload] = wanted


def select_kernel(asked_ref, have_ref, out_ref):
    payload = out_ref.shape[1]
    tasks = out_ref.shape[0] // GROUP
    yh = lax.rem(lax.div(lax.axis_index("wide"), NEAR), YH)
    for j in range(GROUP):
        x, near = divmod(j, NEAR)
        w = (x * YH + yh) * NEAR + near
        for s in range(tasks):
            out_ref[j * tasks + s] = have_ref[asked_ref[w * tasks + s], :payload]


def ladder_kernel(shape_ref, rows_ref, integrals_ref, needed_ref, out_ref):
    tasks, width, depth = integrals_ref.shape
    members, per, _, _ = needed_ref.shape
    halves = depth // members // LANES
    duos = per // tasks // halves
    pairs = 2 * duos
    out_ref[...] = jnp.zeros_like(out_ref)
    for t in range(tasks):
        chosen = [
            needed_ref[j, (t * halves + h) * duos : (t * halves + h + 1) * duos].reshape(pairs, LANES)
            for j in range(members)
            for h in range(halves)
        ]
        product = lax.dot_general(
            jnp.concatenate(chosen, axis=1),
            integrals_ref[t],
            (((1,), (1,)), ((), ())),
            preferred_element_type=jnp.float32,
        )
        live = lax.broadcasted_iota(jnp.int32, product.shape, 1) < shape_ref[t]
        product = jnp.where(live, product, 0.0)
        out_ref[rows_ref[t]] += jnp.concatenate([product[: pairs // 2], product[pairs // 2 :]], axis=1)


def local(integrals, task_shape, task_rows, task_cols, tile_owner, amplitudes):
    tasks, width, depth = integrals.shape
    pairs = amplitudes.shape[1]
    narrow = lax.axis_size("narrow")
    wide = lax.axis_size("wide")
    payload = depth // GROUP // LANES * pairs // 2
    kind = amplitudes.dtype
    groups = [[(x * YH + yh) * NEAR + near for x in range(XS) for near in range(NEAR)] for yh in range(YH)]

    blocks = pl.pallas_call(
        spread_kernel,
        out_shape=jax.ShapeDtypeStruct((wide, payload + 1, 2, LANES), kind),
        in_specs=[ANY, ANY, ANY],
        out_specs=VMEM,
        scratch_shapes=[
            pltpu.SMEM(task_cols.shape, jnp.int32),
            pltpu.SMEM(tile_owner.shape, jnp.int32),
            pltpu.VMEM(amplitudes.shape, kind),
            pltpu.SemaphoreType.DMA((3,)),
        ],
        compiler_params=room(1),
    )(stay(task_cols), stay(tile_owner), stay(amplitudes))
    have = lax.all_to_all(blocks, "wide", 0, 0, tiled=True)

    asked = have[:, payload, 0, :tasks].astype(jnp.int32).reshape(wide * tasks)
    chosen = pl.pallas_call(
        select_kernel,
        out_shape=jax.ShapeDtypeStruct((GROUP * tasks, payload, 2, LANES), kind),
        in_specs=[SMEM, VMEM],
        out_specs=VMEM,
        compiler_params=room(3),
    )(asked, have)
    chosen = chosen.reshape(GROUP, tasks * payload, 2, LANES)
    needed = lax.all_to_all(chosen, "wide", 0, 0, axis_index_groups=groups, tiled=True)

    rows = pl.pallas_call(
        ladder_kernel,
        out_shape=jax.ShapeDtypeStruct((narrow, pairs // 2, 2 * width), jnp.float32),
        in_specs=[SMEM, SMEM, VMEM, VMEM],
        out_specs=VMEM,
        compiler_params=room(1),
    )(task_shape, task_rows, integrals, needed)
    rows = lax.all_to_all(rows, "narrow", 0, 0, tiled=True)
    total = jnp.sum(rows, axis=0)
    return jnp.concatenate([total[:, :width], total[:, width:]], axis=0)


def solution(mesh):
    placed = (
        P(("wide", "narrow"), None, None),
        P(("wide", "narrow")),
        P(("wide", "narrow")),
        P(("wide", "narrow")),
        P(),
        P("wide", None, None),
    )
    return jax.shard_map(
        local, mesh=mesh, in_specs=placed, out_specs=P(None, ("wide", "narrow")), check_vma=False
    )
```

```python
import jax
import jax.numpy as jnp
from jax import lax
from jax.experimental import pallas as pl
from jax.experimental.pallas import tpu as pltpu
from jax.sharding import PartitionSpec as P

XS, YH, YL, CORES = 4, 4, 2, 2
NEAR = YL * CORES
GROUP = XS * NEAR
LANES = 128
ANY = pl.BlockSpec(memory_space=pl.ANY)
VMEM = pl.BlockSpec(memory_space=pltpu.VMEM)
SMEM = pl.BlockSpec(memory_space=pltpu.SMEM)


def room(mib):
    return pltpu.CompilerParams(vmem_limit_bytes=mib * 1024 * 1024)


def stay(x):
    return pltpu.with_memory_space_constraint(x, pltpu.HBM)


def keep(x):
    return pltpu.with_memory_space_constraint(x, pltpu.VMEM)


def spread_kernel(cols_hbm, owner_hbm, amp_hbm, out_ref, cols_ref, owner_ref, amp_ref, sems):
    pairs_of = ((cols_hbm, cols_ref), (owner_hbm, owner_ref), (amp_hbm, amp_ref))
    copies = [pltpu.make_async_copy(src, dst, sems.at[i]) for i, (src, dst) in enumerate(pairs_of)]
    for copy in copies:
        copy.start()
    tasks = cols_ref.shape[0]
    _, pairs, depth = amp_ref.shape
    part = depth // GROUP
    payload = out_ref.shape[1] - 1
    copies[0].wait()
    copies[1].wait()
    lane = lax.broadcasted_iota(jnp.int32, (2, LANES), 1)
    wanted = jnp.zeros((2, LANES), jnp.float32)
    for s in range(tasks):
        wanted = jnp.where(lane == s, owner_ref[cols_ref[s]].astype(jnp.float32), wanted)
    wanted = wanted.astype(out_ref.dtype)
    copies[2].wait()
    for j in range(GROUP):
        x, near = divmod(j, NEAR)
        for h in range(part // LANES):
            at = j * part + h * LANES
            tile = amp_ref[0, :, at : at + LANES].reshape(pairs // 2, 2, LANES)
            for yh in range(YH):
                out_ref[(x * YH + yh) * NEAR + near, h * (pairs // 2) : (h + 1) * (pairs // 2)] = tile
        for yh in range(YH):
            out_ref[(x * YH + yh) * NEAR + near, payload] = wanted


def select_kernel(have_ref, out_ref, vector_ref, asked_ref, sem):
    payload = out_ref.shape[1]
    tasks = out_ref.shape[0] // GROUP
    yh = lax.rem(lax.div(lax.axis_index("wide"), NEAR), YH)
    for j in range(GROUP):
        x, near = divmod(j, NEAR)
        slots = have_ref[(x * YH + yh) * NEAR + near, payload]
        vector_ref[2 * j : 2 * j + 2] = slots.astype(jnp.float32).astype(jnp.int32)
    copy = pltpu.make_async_copy(vector_ref, asked_ref, sem)
    copy.start()
    copy.wait()
    for j in range(GROUP):
        for s in range(tasks):
            out_ref[j * tasks + s] = have_ref[asked_ref[2 * j, s], :payload]


def ladder_kernel(shape_ref, rows_ref, integrals_ref, needed_ref, out_ref):
    tasks, width, depth = integrals_ref.shape
    members, per, _, _ = needed_ref.shape
    halves = depth // members // LANES
    duos = per // tasks // halves
    pairs = 2 * duos
    out_ref[...] = jnp.zeros_like(out_ref)
    for t in range(tasks):
        chosen = [
            needed_ref[j, (t * halves + h) * duos : (t * halves + h + 1) * duos].reshape(pairs, LANES)
            for j in range(members)
            for h in range(halves)
        ]
        product = lax.dot_general(
            jnp.concatenate(chosen, axis=1),
            integrals_ref[t],
            (((1,), (1,)), ((), ())),
            preferred_element_type=jnp.float32,
        )
        live = lax.broadcasted_iota(jnp.int32, product.shape, 1) < shape_ref[t]
        product = jnp.where(live, product, 0.0)
        out_ref[rows_ref[t]] += jnp.concatenate([product[: pairs // 2], product[pairs // 2 :]], axis=1)


def local(integrals, task_shape, task_rows, task_cols, tile_owner, amplitudes):
    tasks, width, depth = integrals.shape
    pairs = amplitudes.shape[1]
    narrow = lax.axis_size("narrow")
    wide = lax.axis_size("wide")
    payload = depth // GROUP // LANES * pairs // 2
    kind = amplitudes.dtype
    groups = [[(x * YH + yh) * NEAR + near for x in range(XS) for near in range(NEAR)] for yh in range(YH)]

    blocks = pl.pallas_call(
        spread_kernel,
        out_shape=jax.ShapeDtypeStruct((wide, payload + 1, 2, LANES), kind),
        in_specs=[ANY, ANY, ANY],
        out_specs=VMEM,
        scratch_shapes=[
            pltpu.SMEM(task_cols.shape, jnp.int32),
            pltpu.SMEM(tile_owner.shape, jnp.int32),
            pltpu.VMEM(amplitudes.shape, kind),
            pltpu.SemaphoreType.DMA((3,)),
        ],
        compiler_params=room(1),
    )(stay(task_cols), stay(tile_owner), stay(amplitudes))
    have = lax.all_to_all(blocks, "wide", 0, 0, tiled=True)

    chosen = pl.pallas_call(
        select_kernel,
        out_shape=jax.ShapeDtypeStruct((GROUP * tasks, payload, 2, LANES), kind),
        in_specs=[VMEM],
        out_specs=VMEM,
        scratch_shapes=[
            pltpu.VMEM((2 * GROUP, LANES), jnp.int32),
            pltpu.SMEM((2 * GROUP, LANES), jnp.int32),
            pltpu.SemaphoreType.DMA,
        ],
        compiler_params=room(1),
    )(have)
    chosen = chosen.reshape(GROUP, tasks * payload, 2, LANES)
    needed = lax.all_to_all(chosen, "wide", 0, 0, axis_index_groups=groups, tiled=True)

    rows = pl.pallas_call(
        ladder_kernel,
        out_shape=jax.ShapeDtypeStruct((narrow, pairs // 2, 2 * width), jnp.float32),
        in_specs=[SMEM, SMEM, VMEM, VMEM],
        out_specs=VMEM,
        compiler_params=room(1),
    )(task_shape, task_rows, integrals, needed)
    rows = lax.all_to_all(rows, "narrow", 0, 0, tiled=True)
    total = jnp.sum(rows, axis=0)
    return jnp.concatenate([total[:, :width], total[:, width:]], axis=0)


def solution(mesh):
    placed = (
        P(("wide", "narrow"), None, None),
        P(("wide", "narrow")),
        P(("wide", "narrow")),
        P(("wide", "narrow")),
        P(),
        P("wide", None, None),
    )
    return jax.shard_map(
        local, mesh=mesh, in_specs=placed, out_specs=P(None, ("wide", "narrow")), check_vma=False
    )
```

```python
import jax
import jax.numpy as jnp
from jax import lax
from jax.experimental import pallas as pl
from jax.experimental.pallas import tpu as pltpu
from jax.sharding import PartitionSpec as P

XS, YH, YL, CORES = 4, 4, 2, 2
NEAR = YL * CORES
GROUP = XS * NEAR
WIDE_FROM, GROUP_FROM, NARROW_FROM = 40, 8, 9
LANES = 128
ANY = pl.BlockSpec(memory_space=pl.ANY)
VMEM = pl.BlockSpec(memory_space=pltpu.VMEM)
SMEM = pl.BlockSpec(memory_space=pltpu.SMEM)


def room(mib):
    return pltpu.CompilerParams(vmem_limit_bytes=mib * 1024 * 1024)


def turned(devices, start):
    return devices[start:] + devices[:start]


def stay(x):
    return pltpu.with_memory_space_constraint(x, pltpu.HBM)


def keep(x):
    return pltpu.with_memory_space_constraint(x, pltpu.VMEM)


def spread_kernel(cols_hbm, owner_hbm, amp_hbm, out_ref, cols_ref, owner_ref, amp_ref, sems):
    pairs_of = ((cols_hbm, cols_ref), (owner_hbm, owner_ref), (amp_hbm, amp_ref))
    copies = [pltpu.make_async_copy(src, dst, sems.at[i]) for i, (src, dst) in enumerate(pairs_of)]
    for copy in copies:
        copy.start()
    tasks = cols_ref.shape[0]
    _, pairs, depth = amp_ref.shape
    part = depth // GROUP
    payload = out_ref.shape[1] - 1
    copies[0].wait()
    copies[1].wait()
    lane = lax.broadcasted_iota(jnp.int32, (2, LANES), 1)
    wanted = jnp.zeros((2, LANES), jnp.float32)
    for s in range(tasks):
        wanted = jnp.where(lane == s, owner_ref[cols_ref[s]].astype(jnp.float32), wanted)
    wanted = wanted.astype(out_ref.dtype)
    copies[2].wait()
    for j in range(GROUP):
        x, near = divmod(j, NEAR)
        places = [((x * YH + yh) * NEAR + near - WIDE_FROM) % out_ref.shape[0] for yh in range(YH)]
        for h in range(part // LANES):
            at = j * part + h * LANES
            tile = amp_ref[0, :, at : at + LANES].reshape(pairs // 2, 2, LANES)
            for place in places:
                out_ref[place, h * (pairs // 2) : (h + 1) * (pairs // 2)] = tile
        for place in places:
            out_ref[place, payload] = wanted


def select_kernel(have_ref, out_ref, vector_ref, asked_ref, sem):
    payload = out_ref.shape[1]
    tasks = out_ref.shape[0] // GROUP
    wide = have_ref.shape[0]
    back = wide - WIDE_FROM
    yh = lax.rem(lax.div(lax.axis_index("wide"), NEAR), YH)
    for j in range(GROUP):
        x, near = divmod(j, NEAR)
        slots = have_ref[lax.rem((x * YH + yh) * NEAR + near + back, wide), payload]
        vector_ref[2 * j : 2 * j + 2] = slots.astype(jnp.float32).astype(jnp.int32)
    copy = pltpu.make_async_copy(vector_ref, asked_ref, sem)
    copy.start()
    copy.wait()
    for j in range(GROUP):
        for s in range(tasks):
            place = (j - GROUP_FROM) % GROUP * tasks + s
            out_ref[place] = have_ref[lax.rem(asked_ref[2 * j, s] + back, wide), :payload]


def ladder_kernel(shape_ref, rows_ref, integrals_ref, needed_ref, out_ref):
    tasks, width, depth = integrals_ref.shape
    members, per, _, _ = needed_ref.shape
    halves = depth // members // LANES
    duos = per // tasks // halves
    pairs = 2 * duos
    narrow = out_ref.shape[0]
    out_ref[...] = jnp.zeros_like(out_ref)
    for t in range(tasks):
        chosen = [
            needed_ref[(j - GROUP_FROM) % members, (t * halves + h) * duos : (t * halves + h + 1) * duos].reshape(pairs, LANES)
            for j in range(members)
            for h in range(halves)
        ]
        product = lax.dot_general(
            jnp.concatenate(chosen, axis=1),
            integrals_ref[t],
            (((1,), (1,)), ((), ())),
            preferred_element_type=jnp.float32,
        )
        live = lax.broadcasted_iota(jnp.int32, product.shape, 1) < shape_ref[t]
        product = jnp.where(live, product, 0.0)
        out_ref[lax.rem(rows_ref[t] + narrow - NARROW_FROM, narrow)] += jnp.concatenate([product[: pairs // 2], product[pairs // 2 :]], axis=1)


def local(integrals, task_shape, task_rows, task_cols, tile_owner, amplitudes):
    tasks, width, depth = integrals.shape
    pairs = amplitudes.shape[1]
    narrow = lax.axis_size("narrow")
    wide = lax.axis_size("wide")
    payload = depth // GROUP // LANES * pairs // 2
    kind = amplitudes.dtype
    groups = [[(x * YH + yh) * NEAR + near for x in range(XS) for near in range(NEAR)] for yh in range(YH)]
    groups = [turned(group, GROUP_FROM) for group in groups]

    blocks = pl.pallas_call(
        spread_kernel,
        out_shape=jax.ShapeDtypeStruct((wide, payload + 1, 2, LANES), kind),
        in_specs=[ANY, ANY, ANY],
        out_specs=VMEM,
        scratch_shapes=[
            pltpu.SMEM(task_cols.shape, jnp.int32),
            pltpu.SMEM(tile_owner.shape, jnp.int32),
            pltpu.VMEM(amplitudes.shape, kind),
            pltpu.SemaphoreType.DMA((3,)),
        ],
        compiler_params=room(1),
    )(stay(task_cols), stay(tile_owner), stay(amplitudes))
    everyone = [turned(list(range(wide)), WIDE_FROM)]
    have = lax.all_to_all(blocks, "wide", 0, 0, axis_index_groups=everyone, tiled=True)

    chosen = pl.pallas_call(
        select_kernel,
        out_shape=jax.ShapeDtypeStruct((GROUP * tasks, payload, 2, LANES), kind),
        in_specs=[VMEM],
        out_specs=VMEM,
        scratch_shapes=[
            pltpu.VMEM((2 * GROUP, LANES), jnp.int32),
            pltpu.SMEM((2 * GROUP, LANES), jnp.int32),
            pltpu.SemaphoreType.DMA,
        ],
        compiler_params=room(1),
    )(have)
    chosen = chosen.reshape(GROUP, tasks * payload, 2, LANES)
    needed = lax.all_to_all(chosen, "wide", 0, 0, axis_index_groups=groups, tiled=True)

    rows = pl.pallas_call(
        ladder_kernel,
        out_shape=jax.ShapeDtypeStruct((narrow, pairs // 2, 2 * width), jnp.float32),
        in_specs=[SMEM, SMEM, VMEM, VMEM],
        out_specs=VMEM,
        compiler_params=room(1),
    )(task_shape, task_rows, integrals, needed)
    column = [turned(list(range(narrow)), NARROW_FROM)]
    rows = lax.all_to_all(rows, "narrow", 0, 0, axis_index_groups=column, tiled=True)
    total = jnp.sum(rows, axis=0)
    return jnp.concatenate([total[:, :width], total[:, width:]], axis=0)


def solution(mesh):
    placed = (
        P(("wide", "narrow"), None, None),
        P(("wide", "narrow")),
        P(("wide", "narrow")),
        P(("wide", "narrow")),
        P(),
        P("wide", None, None),
    )
    return jax.shard_map(
        local, mesh=mesh, in_specs=placed, out_specs=P(None, ("wide", "narrow")), check_vma=False
    )
```

```python
import jax
import jax.numpy as jnp
from jax import lax
from jax.experimental import pallas as pl
from jax.experimental.pallas import tpu as pltpu
from jax.sharding import PartitionSpec as P

XS, YH, YL, CORES = 4, 4, 2, 2
NEAR = YL * CORES
GROUP = XS * NEAR
WIDE_FROM, GROUP_FROM, NARROW_FROM = 41, 9, 9
PIECES = 4
LANES = 128
ANY = pl.BlockSpec(memory_space=pl.ANY)
VMEM = pl.BlockSpec(memory_space=pltpu.VMEM)
SMEM = pl.BlockSpec(memory_space=pltpu.SMEM)


def room(mib):
    return pltpu.CompilerParams(vmem_limit_bytes=mib * 1024 * 1024)


def turned(devices, start):
    return devices[start:] + devices[:start]


def stay(x):
    return pltpu.with_memory_space_constraint(x, pltpu.HBM)


def keep(x):
    return pltpu.with_memory_space_constraint(x, pltpu.VMEM)


def spread_kernel(cols_hbm, owner_hbm, amp_hbm, out_ref, cols_ref, owner_ref, amp_ref, sems):
    width = amp_ref.shape[2] // PIECES
    spans = [pl.ds(i * width, width) for i in range(PIECES)]
    pairs_of = [(cols_hbm, cols_ref), (owner_hbm, owner_ref)]
    pairs_of += [(amp_hbm.at[:, :, span], amp_ref.at[:, :, span]) for span in spans]
    copies = [pltpu.make_async_copy(src, dst, sems.at[i]) for i, (src, dst) in enumerate(pairs_of)]
    for copy in copies:
        copy.start()
    tasks = cols_ref.shape[0]
    _, pairs, depth = amp_ref.shape
    part = depth // GROUP
    payload = out_ref.shape[1] - 1
    copies[0].wait()
    copies[1].wait()
    lane = lax.broadcasted_iota(jnp.int32, (2, LANES), 1)
    wanted = jnp.zeros((2, LANES), jnp.float32)
    for s in range(tasks):
        wanted = jnp.where(lane == s, owner_ref[cols_ref[s]].astype(jnp.float32), wanted)
    wanted = wanted.astype(out_ref.dtype)
    for j in range(GROUP):
        if j % (GROUP // PIECES) == 0:
            copies[2 + j * PIECES // GROUP].wait()
        x, near = divmod(j, NEAR)
        places = [((x * YH + yh) * NEAR + near - WIDE_FROM) % out_ref.shape[0] for yh in range(YH)]
        for h in range(part // LANES):
            at = j * part + h * LANES
            tile = amp_ref[0, :, at : at + LANES].reshape(pairs // 2, 2, LANES)
            for place in places:
                out_ref[place, h * (pairs // 2) : (h + 1) * (pairs // 2)] = tile
        for place in places:
            out_ref[place, payload] = wanted


def select_kernel(have_ref, out_ref, vector_ref, asked_ref, sem):
    payload = out_ref.shape[1]
    tasks = out_ref.shape[0] // GROUP
    wide = have_ref.shape[0]
    back = wide - WIDE_FROM
    yh = lax.rem(lax.div(lax.axis_index("wide"), NEAR), YH)
    for j in range(GROUP):
        x, near = divmod(j, NEAR)
        slots = have_ref[lax.rem((x * YH + yh) * NEAR + near + back, wide), payload]
        slots = slots.astype(jnp.float32).astype(jnp.int32) + back
        vector_ref[2 * j : 2 * j + 2] = jnp.where(slots < wide, slots, slots - wide)
    copy = pltpu.make_async_copy(vector_ref, asked_ref, sem)
    copy.start()
    copy.wait()
    for j in range(GROUP):
        for s in range(tasks):
            place = (j - GROUP_FROM) % GROUP * tasks + s
            out_ref[place] = have_ref[asked_ref[2 * j, s], :payload]


def ladder_kernel(shape_ref, rows_ref, integrals_ref, needed_ref, out_ref):
    tasks, width, depth = integrals_ref.shape
    members, per, _, _ = needed_ref.shape
    halves = depth // members // LANES
    duos = per // tasks // halves
    pairs = 2 * duos
    narrow = out_ref.shape[0]
    out_ref[...] = jnp.zeros_like(out_ref)
    for t in range(tasks):
        chosen = [
            needed_ref[(j - GROUP_FROM) % members, (t * halves + h) * duos : (t * halves + h + 1) * duos].reshape(pairs, LANES)
            for j in range(members)
            for h in range(halves)
        ]
        product = lax.dot_general(
            jnp.concatenate(chosen, axis=1),
            integrals_ref[t],
            (((1,), (1,)), ((), ())),
            preferred_element_type=jnp.float32,
        )
        live = lax.broadcasted_iota(jnp.int32, product.shape, 1) < shape_ref[t]
        product = jnp.where(live, product, 0.0)
        out_ref[lax.rem(rows_ref[t] + narrow - NARROW_FROM, narrow)] += jnp.concatenate([product[: pairs // 2], product[pairs // 2 :]], axis=1)


def local(integrals, task_shape, task_rows, task_cols, tile_owner, amplitudes):
    tasks, width, depth = integrals.shape
    pairs = amplitudes.shape[1]
    narrow = lax.axis_size("narrow")
    wide = lax.axis_size("wide")
    payload = depth // GROUP // LANES * pairs // 2
    kind = amplitudes.dtype
    groups = [[(x * YH + yh) * NEAR + near for x in range(XS) for near in range(NEAR)] for yh in range(YH)]
    groups = [turned(group, GROUP_FROM) for group in groups]

    blocks = pl.pallas_call(
        spread_kernel,
        out_shape=jax.ShapeDtypeStruct((wide, payload + 1, 2, LANES), kind),
        in_specs=[ANY, ANY, ANY],
        out_specs=VMEM,
        scratch_shapes=[
            pltpu.SMEM(task_cols.shape, jnp.int32),
            pltpu.SMEM(tile_owner.shape, jnp.int32),
            pltpu.VMEM(amplitudes.shape, kind),
            pltpu.SemaphoreType.DMA((2 + PIECES,)),
        ],
        compiler_params=room(1),
    )(stay(task_cols), stay(tile_owner), stay(amplitudes))
    everyone = [turned(list(range(wide)), WIDE_FROM)]
    have = lax.all_to_all(blocks, "wide", 0, 0, axis_index_groups=everyone, tiled=True)

    chosen = pl.pallas_call(
        select_kernel,
        out_shape=jax.ShapeDtypeStruct((GROUP * tasks, payload, 2, LANES), kind),
        in_specs=[VMEM],
        out_specs=VMEM,
        scratch_shapes=[
            pltpu.VMEM((2 * GROUP, LANES), jnp.int32),
            pltpu.SMEM((2 * GROUP, LANES), jnp.int32),
            pltpu.SemaphoreType.DMA,
        ],
        compiler_params=room(1),
    )(have)
    chosen = chosen.reshape(GROUP, tasks * payload, 2, LANES)
    needed = lax.all_to_all(chosen, "wide", 0, 0, axis_index_groups=groups, tiled=True)

    rows = pl.pallas_call(
        ladder_kernel,
        out_shape=jax.ShapeDtypeStruct((narrow, pairs // 2, 2 * width), jnp.float32),
        in_specs=[SMEM, SMEM, VMEM, VMEM],
        out_specs=VMEM,
        compiler_params=room(1),
    )(task_shape, task_rows, integrals, needed)
    column = [turned(list(range(narrow)), NARROW_FROM)]
    rows = lax.all_to_all(rows, "narrow", 0, 0, axis_index_groups=column, tiled=True)
    total = jnp.sum(rows, axis=0)
    return jnp.concatenate([total[:, :width], total[:, width:]], axis=0)


def solution(mesh):
    placed = (
        P(("wide", "narrow"), None, None),
        P(("wide", "narrow")),
        P(("wide", "narrow")),
        P(("wide", "narrow")),
        P(),
        P("wide", None, None),
    )
    return jax.shard_map(
        local, mesh=mesh, in_specs=placed, out_specs=P(None, ("wide", "narrow")), check_vma=False
    )
```

```python
import jax
import jax.numpy as jnp
from jax import lax
from jax.experimental import pallas as pl
from jax.experimental.pallas import tpu as pltpu
from jax.sharding import PartitionSpec as P

XS, YH, YL, CORES = 4, 4, 2, 2
NEAR = YL * CORES
GROUP = XS * NEAR
WIDE_FROM, GROUP_FROM, NARROW_FROM = 41, 9, 9
PIECES = 4
LANES = 128
ANY = pl.BlockSpec(memory_space=pl.ANY)
VMEM = pl.BlockSpec(memory_space=pltpu.VMEM)
SMEM = pl.BlockSpec(memory_space=pltpu.SMEM)


def room(mib):
    return pltpu.CompilerParams(vmem_limit_bytes=mib * 1024 * 1024)


def turned(devices, start):
    return devices[start:] + devices[:start]


def stay(x):
    return pltpu.with_memory_space_constraint(x, pltpu.HBM)


def keep(x):
    return pltpu.with_memory_space_constraint(x, pltpu.VMEM)


def spread_kernel(cols_hbm, owner_hbm, amp_hbm, out_ref, cols_ref, owner_ref, amp_ref, sems):
    width = amp_ref.shape[2] // PIECES
    spans = [pl.ds(i * width, width) for i in range(PIECES)]
    pairs_of = [(cols_hbm, cols_ref), (owner_hbm, owner_ref)]
    pairs_of += [(amp_hbm.at[:, :, span], amp_ref.at[:, :, span]) for span in spans]
    copies = [pltpu.make_async_copy(src, dst, sems.at[i]) for i, (src, dst) in enumerate(pairs_of)]
    for copy in copies:
        copy.start()
    tasks = cols_ref.shape[0]
    _, pairs, depth = amp_ref.shape
    part = depth // GROUP
    payload = out_ref.shape[1] - 1
    copies[0].wait()
    copies[1].wait()
    lane = lax.broadcasted_iota(jnp.int32, (2, LANES), 1)
    wanted = jnp.zeros((2, LANES), jnp.float32)
    for s in range(tasks):
        wanted = jnp.where(lane % tasks == s, owner_ref[cols_ref[s]].astype(jnp.float32), wanted)
    wanted = wanted.astype(out_ref.dtype)
    for j in range(GROUP):
        if j % (GROUP // PIECES) == 0:
            copies[2 + j * PIECES // GROUP].wait()
        x, near = divmod(j, NEAR)
        places = [((x * YH + yh) * NEAR + near - WIDE_FROM) % out_ref.shape[0] for yh in range(YH)]
        for h in range(part // LANES):
            at = j * part + h * LANES
            tile = amp_ref[0, :, at : at + LANES].reshape(pairs // 2, 2, LANES)
            for place in places:
                out_ref[place, h * (pairs // 2) : (h + 1) * (pairs // 2)] = tile
        for place in places:
            out_ref[place, payload] = wanted


def select_kernel(have_ref, out_ref, vector_ref, asked_ref, sem):
    payload = out_ref.shape[1]
    tasks = out_ref.shape[0] // GROUP
    wide = have_ref.shape[0]
    back = wide - WIDE_FROM
    yh = lax.rem(lax.div(lax.axis_index("wide"), NEAR), YH)
    member = lax.broadcasted_iota(jnp.int32, (2, LANES), 1) // tasks
    asked = jnp.zeros((2, LANES), jnp.float32)
    for j in range(GROUP):
        x, near = divmod(j, NEAR)
        slots = have_ref[lax.rem((x * YH + yh) * NEAR + near + back, wide), payload]
        asked = jnp.where(member == j, slots.astype(jnp.float32), asked)
    asked = asked.astype(jnp.int32) + back
    vector_ref[...] = jnp.where(asked < wide, asked, asked - wide)
    copy = pltpu.make_async_copy(vector_ref, asked_ref, sem)
    copy.start()
    copy.wait()
    for j in range(GROUP):
        for s in range(tasks):
            place = (j - GROUP_FROM) % GROUP * tasks + s
            out_ref[place] = have_ref[asked_ref[0, j * tasks + s], :payload]


def ladder_kernel(shape_ref, rows_ref, integrals_ref, needed_ref, out_ref):
    tasks, width, depth = integrals_ref.shape
    members, per, _, _ = needed_ref.shape
    halves = depth // members // LANES
    duos = per // tasks // halves
    pairs = 2 * duos
    narrow = out_ref.shape[0]
    out_ref[...] = jnp.zeros_like(out_ref)
    for t in range(tasks):
        chosen = [
            needed_ref[(j - GROUP_FROM) % members, (t * halves + h) * duos : (t * halves + h + 1) * duos].reshape(pairs, LANES)
            for j in range(members)
            for h in range(halves)
        ]
        product = lax.dot_general(
            jnp.concatenate(chosen, axis=1),
            integrals_ref[t],
            (((1,), (1,)), ((), ())),
            preferred_element_type=jnp.float32,
        )
        live = lax.broadcasted_iota(jnp.int32, product.shape, 1) < shape_ref[t]
        product = jnp.where(live, product, 0.0)
        out_ref[lax.rem(rows_ref[t] + narrow - NARROW_FROM, narrow)] += jnp.concatenate([product[: pairs // 2], product[pairs // 2 :]], axis=1)


def local(integrals, task_shape, task_rows, task_cols, tile_owner, amplitudes):
    tasks, width, depth = integrals.shape
    pairs = amplitudes.shape[1]
    narrow = lax.axis_size("narrow")
    wide = lax.axis_size("wide")
    payload = depth // GROUP // LANES * pairs // 2
    kind = amplitudes.dtype
    groups = [[(x * YH + yh) * NEAR + near for x in range(XS) for near in range(NEAR)] for yh in range(YH)]
    groups = [turned(group, GROUP_FROM) for group in groups]

    blocks = pl.pallas_call(
        spread_kernel,
        out_shape=jax.ShapeDtypeStruct((wide, payload + 1, 2, LANES), kind),
        in_specs=[ANY, ANY, ANY],
        out_specs=VMEM,
        scratch_shapes=[
            pltpu.SMEM(task_cols.shape, jnp.int32),
            pltpu.SMEM(tile_owner.shape, jnp.int32),
            pltpu.VMEM(amplitudes.shape, kind),
            pltpu.SemaphoreType.DMA((2 + PIECES,)),
        ],
        compiler_params=room(1),
    )(stay(task_cols), stay(tile_owner), stay(amplitudes))
    everyone = [turned(list(range(wide)), WIDE_FROM)]
    have = lax.all_to_all(blocks, "wide", 0, 0, axis_index_groups=everyone, tiled=True)

    chosen = pl.pallas_call(
        select_kernel,
        out_shape=jax.ShapeDtypeStruct((GROUP * tasks, payload, 2, LANES), kind),
        in_specs=[VMEM],
        out_specs=VMEM,
        scratch_shapes=[
            pltpu.VMEM((2, GROUP * tasks), jnp.int32),
            pltpu.SMEM((2, GROUP * tasks), jnp.int32),
            pltpu.SemaphoreType.DMA,
        ],
        compiler_params=room(1),
    )(have)
    chosen = chosen.reshape(GROUP, tasks * payload, 2, LANES)
    needed = lax.all_to_all(chosen, "wide", 0, 0, axis_index_groups=groups, tiled=True)

    rows = pl.pallas_call(
        ladder_kernel,
        out_shape=jax.ShapeDtypeStruct((narrow, pairs // 2, 2 * width), jnp.float32),
        in_specs=[SMEM, SMEM, VMEM, VMEM],
        out_specs=VMEM,
        compiler_params=room(1),
    )(task_shape, task_rows, integrals, needed)
    column = [turned(list(range(narrow)), NARROW_FROM)]
    rows = lax.all_to_all(rows, "narrow", 0, 0, axis_index_groups=column, tiled=True)
    total = jnp.sum(rows, axis=0)
    return jnp.concatenate([total[:, :width], total[:, width:]], axis=0)


def solution(mesh):
    placed = (
        P(("wide", "narrow"), None, None),
        P(("wide", "narrow")),
        P(("wide", "narrow")),
        P(("wide", "narrow")),
        P(),
        P("wide", None, None),
    )
    return jax.shard_map(
        local, mesh=mesh, in_specs=placed, out_specs=P(None, ("wide", "narrow")), check_vma=False
    )
```
